256 devices in a mesh: blk: 64 (over x, z, y_hi), col: 4 (over y_lo, core).
Axes of the slice: x: 4, y: 4 (y_hi: 2, y_lo: 2; y = y_hi * 2 + y_lo), z: 8, core: 2. Of those that a mesh axis runs over, the one named last changes fastest.
Arguments:
- node_features: bfloat16 [131072, 128], P(('blk', 'col')), may hold values from -6 to 6
- degree: int32 [131072], P(('blk', 'col')), may hold values from 1 to 8
- adjacency: bfloat16 [92160, 128, 128], P(('blk', 'col')), may hold values from -0.125 to 0.125
- tile_rows: int32 [92160], P(('blk', 'col')), may hold values from 0 to 15
- tile_cols: int32 [92160], P(('blk', 'col')), may hold values from 0 to 3
- counts: int32 [1280], P(('blk', 'col')), may hold values from 1 to 72, as said below
- weight: bfloat16 [128, 256], replicated, may hold values from -0.5 to 0.5
- bias_vector: float32 [256], replicated, may hold values from -3 to 3
- cotangent: bfloat16 [131072, 256], P(('blk', 'col')), may hold values from -6 to 6
Outputs:
- activations: bfloat16 [131072, 256], P(('blk', 'col'))
- grad_features: bfloat16 [131072, 128], P(('blk', 'col'))
- grad_weight: float32 [128, 256], replicated
- grad_bias: float32 [256], replicated
The draws below stay inside these ranges and needn't reach their ends.
Inputs may be any that keep to these rules, and one draw needn't show every extreme that they name: `counts`: every draw has some pair with all 72 slots live.
All inputs are finite; a program needn't handle non-finite values.
Results may differ from the reference program's by a relative error of at most 0.012.
Values may be sent and summed in bfloat16 or wider, within the bound.
A program may use at most 128 MiB of HBM per device.

```python
import jax
import jax.numpy as jnp
from jax import lax

FIN = 128
FH = 256
TILE = 128
DEV_TILES = 4
REACH = 2
SPAN = 5
SLOTS = 72
BLOCK_TILES = 16
NODES = 131072
PAIRS = 1280
N_BLK = 64
N_COL = 4


def draw_counts(key, part):
    first_key, second_key, spot_key = jax.random.split(jax.random.fold_in(key, 17), 3)
    first_draw = jax.random.randint(first_key, (PAIRS,), 1, SLOTS + 1)
    second_draw = jax.random.randint(second_key, (PAIRS,), 1, SLOTS + 1)
    larger_counts = jnp.maximum(first_draw, second_draw)
    spot_index = jax.random.randint(spot_key, (), 0, PAIRS)
    return larger_counts.at[spot_index].set(SLOTS).astype(jnp.int32)


def with_ends(drawn, stream_key, smallest, high):
    longest = drawn.shape.index(max(drawn.shape))
    spots = []
    for shift in (0, 1):
        where = [jax.random.randint(jax.random.fold_in(stream_key, axis), (), 0, length) for axis, length in enumerate(drawn.shape)]
        where[longest] = (where[longest] + shift) % drawn.shape[longest]
        spots.append(tuple(where))
    return drawn.at[spots[0]].set(smallest).at[spots[1]].set(high)


def level_of(stream_key, extent, pieces, smallest, high):
    loudness = 1.0
    for dim, blocks in pieces:
        steps = jax.random.uniform(jax.random.fold_in(jax.random.fold_in(stream_key, 6), dim), (blocks,), jnp.float32, smallest / len(pieces), high / len(pieces))
        loudness = loudness * jnp.repeat(jnp.exp(steps), extent[dim] // blocks).reshape((-1,) + (1,) * (len(extent) - 1 - dim))
    return loudness


def normal_values(own_key, shape, deviation, reach, pieces=(), held_as=jnp.bfloat16):
    values = jax.random.normal(own_key, shape, jnp.float32) * deviation
    if len(pieces) > 0:
        values = level_of(own_key, shape, pieces, -0.22, 0.18) * values
    return jnp.clip(values, min=-reach, max=reach).astype(held_as)


def setup_inputs(seed: int = 0) -> dict:
    arg_keys = jax.random.split(jax.random.key(seed), 10)
    return {
        "node_features": normal_values(arg_keys[0], (NODES, FIN), 1.0, 6.0, ((0, 256),)),
        "degree": with_ends(jax.random.randint(arg_keys[1], (NODES,), 1, 9), jax.random.fold_in(arg_keys[1], 1), 1, 8).astype(jnp.int32),
        "adjacency": normal_values(arg_keys[2], (PAIRS * SLOTS, TILE, TILE), (4 * SPAN * TILE) ** -0.5, 0.125, ((0, 256),)),
        "tile_rows": with_ends(jax.random.randint(arg_keys[3], (PAIRS * SLOTS,), 0, BLOCK_TILES), jax.random.fold_in(arg_keys[3], 1), 0, BLOCK_TILES - 1).astype(jnp.int32),
        "tile_cols": with_ends(jax.random.randint(arg_keys[4], (PAIRS * SLOTS,), 0, DEV_TILES), jax.random.fold_in(arg_keys[4], 1), 0, DEV_TILES - 1).astype(jnp.int32),
        "counts": draw_counts(jax.random.fold_in(arg_keys[9], 71), 0),
        "weight": normal_values(arg_keys[6], (FIN, FH), FIN ** -0.5, 0.5),
        "bias_vector": normal_values(arg_keys[7], (FH,), 0.5, 3.0, (), jnp.float32),
        "cotangent": normal_values(arg_keys[8], (NODES, FH), 1.0, 6.0, ((0, 256),)),
    }


def reference(node_features, degree, adjacency, tile_rows, tile_cols, counts, weight, bias_vector, cotangent):
    offset_count = 2 * REACH + 1
    block_count = N_COL * DEV_TILES
    row_scale = lax.rsqrt(degree.astype(jnp.float32))
    source = (row_scale[:, None] * node_features.astype(jnp.float32)).astype(jnp.bfloat16)
    source_parts = source.reshape(N_BLK, N_COL, DEV_TILES, TILE, FIN)
    tile_parts = adjacency.reshape(N_BLK, N_COL, offset_count, SLOTS, TILE, TILE)
    rows_parts = tile_rows.reshape(N_BLK, N_COL, offset_count, SLOTS).astype(jnp.int32)
    cols_parts = tile_cols.reshape(N_BLK, N_COL, offset_count, SLOTS).astype(jnp.int32)
    slot_index = jnp.arange(SLOTS).astype(jnp.int32)
    live_slots = (slot_index[None, None, None, :] < counts.reshape(N_BLK, N_COL, offset_count)[..., None]).astype(jnp.float32)
    col_index = jnp.arange(N_COL).astype(jnp.int32).reshape(N_COL, 1, 1)
    block_index = jnp.arange(N_BLK).astype(jnp.int32)

    def source_blocks(block):
        shifted = (block + jnp.arange(offset_count).astype(jnp.int32) - REACH) % N_BLK
        return shifted.astype(jnp.int32).reshape(1, offset_count, 1)

    def forward_block(block):
        picked = source_parts[source_blocks(block), col_index, cols_parts[block]]
        products = jnp.einsum('cksrq,cksqf->cksrf', tile_parts[block].astype(jnp.float32), picked.astype(jnp.float32))
        products = products * live_slots[block][..., None, None]
        summed = jax.ops.segment_sum(products.reshape(-1, TILE, FIN), rows_parts[block].reshape(-1), block_count)
        return summed.reshape(block_count * TILE, FIN)
    sums = lax.map(forward_block, block_index).reshape(NODES, FIN)
    aggregated = (row_scale[:, None] * sums).astype(jnp.bfloat16)
    pre_act = jnp.dot(aggregated, weight, preferred_element_type=jnp.float32) + bias_vector.astype(jnp.float32)
    gate_value = jax.nn.sigmoid(pre_act)
    activations = (pre_act * gate_value).astype(jnp.bfloat16)
    grad_pre = cotangent.astype(jnp.float32) * gate_value * (1.0 + pre_act * (1.0 - gate_value))
    grad_low = grad_pre.astype(jnp.bfloat16)
    norm_factor = float(NODES) ** (-0.5)
    grad_weight = jnp.dot(aggregated.T, grad_low, preferred_element_type=jnp.float32) * norm_factor
    grad_bias = lax.optimization_barrier(jnp.sum(grad_pre, axis=0)) * norm_factor
    grad_rows = jnp.dot(grad_low, weight.T, preferred_element_type=jnp.float32)
    grad_hidden = (row_scale[:, None] * grad_rows).astype(jnp.bfloat16)
    hidden_parts = grad_hidden.reshape(N_BLK, block_count, TILE, FIN)

    def backward_block(accum, block):
        picked = hidden_parts[block][rows_parts[block]]
        back_terms = jnp.einsum('cksrq,cksrf->cksqf', tile_parts[block].astype(jnp.float32), picked.astype(jnp.float32))
        back_terms = back_terms * live_slots[block][..., None, None]
        accum = accum.at[source_blocks(block), col_index, cols_parts[block]].add(back_terms)
        return (accum, None)
    start_accum = jnp.zeros((N_BLK, N_COL, DEV_TILES, TILE, FIN), jnp.float32)
    back_sums, _ = lax.scan(backward_block, start_accum, block_index)
    back_sums = back_sums.reshape(NODES, FIN)
    grad_features = (row_scale[:, None] * back_sums).astype(jnp.bfloat16)
    return (activations, grad_features, grad_weight, grad_bias)
```

```python
import functools

import jax
import jax.numpy as jnp
from jax import lax
from jax.experimental import pallas as pl
from jax.experimental.pallas import tpu as pltpu
from jax.sharding import PartitionSpec as P

F32 = jnp.float32
BF16 = jnp.bfloat16
MESH = pl.DeviceIdType.MESH
COLS = 4
HI = 2
ZLEN = 8


def remote(src, dst, send_sem, recv_sem, blk, col):
    return pltpu.make_async_remote_copy(
        src_ref=src,
        dst_ref=dst,
        send_sem=send_sem,
        recv_sem=recv_sem,
        device_id={"blk": blk, "col": col},
        device_id_type=MESH,
    )


def loop(count, body):
    def step(i, carry):
        body(i)
        return carry

    lax.fori_loop(0, count, step, 0)


def kernel(
    n_blk,
    n_z,
    norm,
    prev,
    last,
    feats,
    deg,
    adj,
    weight,
    bias,
    cot,
    act_out,
    gf_out,
    gw_out,
    gb_out,
    tiles,
    chain,
    dense,
    feat_v,
    weight_v,
    cot_v,
    act_v,
    scale_col,
    source,
    own_sum,
    rs_send,
    rs_recv,
    hidden,
    back,
    back_send,
    back_recv,
    r1_send,
    r1_recv,
    r2_send,
    r2_recv,
    r3_recv,
    g1,
    g2,
    in_sem,
    tile_sem,
    act_sem,
    src_ss,
    src_rs,
    rs_ss,
    rs_rs,
    hid_ss,
    hid_rs,
    back_ss,
    back_rs,
    r1_ss,
    r1_rs,
    r2_ss,
    r2_rs,
    r3_ss,
    r3_rs,
    g1_ss,
    g1_rs,
    g2_ss,
    g2_rs,
):
    span, slots, tile, _ = tiles.shape
    reach = span // 2
    rows, fin = feats.shape
    dev_tiles = rows // tile
    block_tiles = COLS * dev_tiles
    n_xy = n_blk // n_z

    blk = lax.axis_index("blk")
    col = lax.axis_index("col")
    hi = blk % HI
    z = (blk // HI) % n_z
    xy = (blk // (HI * n_z)) * HI + hi

    def block_at(z_, xy_):
        return ((xy_ // HI) * n_z + z_) * HI + xy_ % HI

    def near(k):
        return (blk + k - reach + n_blk) % n_blk

    mates = [(col + 2) % COLS, COLS - 1 - col, col + 1 - 2 * (col % 2)]

    copies_in = [
        pltpu.make_async_copy(feats, feat_v, in_sem.at[0]),
        pltpu.make_async_copy(weight, weight_v, in_sem.at[1]),
        pltpu.make_async_copy(cot, cot_v, in_sem.at[2]),
    ]
    copies_in[0].start()

    def tile_copy(k):
        return pltpu.make_async_copy(adj.at[pl.ds(k * slots, slots)], tiles.at[k], tile_sem.at[k])

    loop(span, lambda k: tile_copy(k).start())
    copies_in[1].start()
    copies_in[2].start()

    barrier = pltpu.get_barrier_semaphore()

    def hello(b, c):
        pl.semaphore_signal(barrier, inc=1, device_id={"blk": b, "col": c}, device_id_type=MESH)

    for k in range(span):
        if k != reach:
            hello(near(k), col)
    for mate in mates:
        hello(blk, mate)
    loop(n_z - 1, lambda i: hello(block_at((z + 1 + i) % n_z, xy), col))
    loop(n_xy - 1, lambda i: hello(block_at(z, (xy + 1 + i) % n_xy), col))

    scale_row = lax.rsqrt(deg[...].astype(F32))
    scale_col[...] = jnp.transpose(jnp.broadcast_to(scale_row, (fin, rows)))
    copies_in[0].wait()
    source[reach] = (scale_col[...] * feat_v[...].astype(F32)).astype(BF16)
    chain[slots] = jnp.zeros((tile, tile), F32)

    pl.semaphore_wait(barrier, (span - 1) + (COLS - 1) + (n_z - 1) + (n_xy - 1))

    sends = []
    for k in (1, 3, 0, 4):
        sends.append(
            remote(source.at[reach], source.at[k], src_ss.at[k], src_rs.at[k], near(span - 1 - k), col)
        )
        sends[-1].start()
    arrivals = list(sends)

    def build(k):
        tile_copy(k).wait()

        def slot(s):
            chain[s] = tiles[k, s].astype(F32) + chain[prev[k * slots + s]]

        loop(slots, slot)

        def row(r):
            cells = [
                chain[last[(k * block_tiles + r) * dev_tiles + c]].astype(BF16)
                for c in range(dev_tiles)
            ]
            dense[k, pl.ds(r * tile, tile), :] = jnp.concatenate(cells, axis=1)

        loop(block_tiles, row)

    loop(span, build)

    for copy in arrivals:
        copy.wait_recv()

    def chunk_sum(j):
        total = jnp.zeros((rows, fin), F32)
        for k in range(span):
            total += jnp.dot(
                dense[k, pl.ds(j * rows, rows), :], source[k], preferred_element_type=F32
            )
        return total

    rs_copies = []
    for d, mate in enumerate(mates):
        rs_send[d] = chunk_sum(mate).astype(BF16)
        copy = remote(rs_send.at[d], rs_recv.at[d], rs_ss.at[d], rs_rs.at[d], blk, mate)
        copy.start()
        rs_copies.append(copy)
    own_sum[...] = chunk_sum(col)
    copies_in[1].wait()
    copies_in[2].wait()
    sums = own_sum[...]
    for d in (2, 0, 1):
        rs_copies[d].wait_recv()
        sums = sums + rs_recv[d].astype(F32)
    sends += rs_copies

    agg = scale_col[...] * sums
    agg_t = jnp.transpose(agg).astype(BF16)
    agg = agg.astype(BF16)
    pre = jnp.dot(agg, weight_v[...], preferred_element_type=F32) + bias[...]
    gate = jax.nn.sigmoid(pre)
    grad_pre = cot_v[...].astype(F32) * gate * (1.0 + pre * (1.0 - gate))
    low = grad_pre.astype(BF16)
    hidden_t = lax.dot_general(
        weight_v[...], low, (((1,), (1,)), ((), ())), preferred_element_type=F32
    )
    hidden[col] = (hidden_t * scale_row).astype(BF16)
    hid_copies = []
    for d, mate in enumerate(mates):
        copy = remote(hidden.at[col], hidden.at[col], hid_ss.at[d], hid_rs.at[col], blk, mate)
        copy.start()
        sends.append(copy)

    def hidden_from(c):
        return remote(hidden.at[c], hidden.at[c], hid_ss.at[0], hid_rs.at[c], blk, c)

    act_v[...] = (pre * gate).astype(BF16)
    act_copy = pltpu.make_async_copy(act_v, act_out, act_sem)
    act_copy.start()

    part = jnp.dot(agg_t, low, preferred_element_type=F32)
    bias_part = jnp.sum(grad_pre, axis=0, keepdims=True)
    half = part.shape[0] // 2
    bias_rows = jnp.concatenate(
        [bias_part[:, :fin], bias_part[:, fin:], jnp.zeros((6, fin), F32)], axis=0
    )
    for c in range(COLS):
        r1_send[c, :half, :] = part[
            (c % 2) * half : (c % 2 + 1) * half, (c // 2) * fin : (c // 2 + 1) * fin
        ]
        r1_send[c, half:, :] = bias_rows
    r1_recv[col] = r1_send[col]
    for d, mate in enumerate(mates):
        copy = remote(r1_send.at[mate], r1_recv.at[col], r1_ss.at[d], r1_rs.at[col], blk, mate)
        copy.start()
        sends.append(copy)

    def back_term(k, c):
        return jnp.dot(
            hidden[c], dense[k, pl.ds(c * rows, rows), :], preferred_element_type=F32
        )

    def back_first(k):
        back[k] = back_term(k, col)

    loop(span, back_first)

    def back_more(c):
        hidden_from(c).wait_recv()

        def one(k):
            back[k] = back[k] + back_term(k, c)

        loop(span, one)

    back_more(mates[2])

    for mate in mates:
        remote(r1_send.at[mate], r1_recv.at[mate], r1_ss.at[0], r1_rs.at[mate], blk, mate).wait_recv()
    total = r1_recv[0] + r1_recv[1] + r1_recv[2] + r1_recv[3]
    piece = half // n_z
    for i in range(n_z):
        r2_send[i, :piece, :] = total[i * piece : (i + 1) * piece]
        r2_send[i, piece:, :] = total[half:]
    r2_recv[z] = r2_send[z]

    def r2_copy(i, mine):
        other = (z + 1 + i) % n_z
        return remote(
            r2_send.at[other],
            r2_recv.at[z if mine else other],
            r2_ss.at[i],
            r2_rs.at[z if mine else other],
            block_at(other, xy),
            col,
        )

    loop(n_z - 1, lambda i: r2_copy(i, True).start())

    back_more(mates[0])

    def r2_wait(i):
        r2_copy(i, False).wait_recv()

    loop(n_z - 1, r2_wait)
    total = r2_recv[0]
    for i in range(1, n_z):
        total = total + r2_recv[i]
    r3_recv[xy] = total

    def r3_copy(i, mine):
        other = (xy + 1 + i) % n_xy
        return remote(
            r3_recv.at[xy],
            r3_recv.at[xy if mine else other],
            r3_ss.at[i],
            r3_rs.at[xy if mine else other],
            block_at(z, other),
            col,
        )

    loop(n_xy - 1, lambda i: r3_copy(i, True).start())

    hidden_from(mates[1]).wait_recv()
    back_copies = []
    for k in (1, 3, 0, 4):
        back_send[k] = (back[k] + back_term(k, mates[1])).astype(BF16)
        copy = remote(
            back_send.at[k], back_recv.at[k], back_ss.at[k], back_rs.at[k], near(k), col
        )
        copy.start()
        back_copies.append(copy)
    own = back[reach] + back_term(reach, mates[1])
    sends += back_copies

    loop(n_xy - 1, lambda i: r3_copy(i, False).wait_recv())
    total = r3_recv[0]
    for i in range(1, n_xy):
        total = total + r3_recv[i]
    g1[z] = total[:piece] * norm
    gb_out[:, :fin] = total[piece : piece + 1] * norm
    gb_out[:, fin:] = total[piece + 1 : piece + 2] * norm

    def g1_copy(i, mine):
        other = (z + 1 + i) % n_z
        return remote(
            g1.at[z],
            g1.at[z if mine else other],
            g1_ss.at[i],
            g1_rs.at[z if mine else other],
            block_at(other, xy),
            col,
        )

    loop(n_z - 1, lambda i: g1_copy(i, True).start())
    back[reach] = own
    loop(n_z - 1, lambda i: g1_copy(i, False).wait_recv())
    g2[col] = jnp.concatenate([g1[i] for i in range(n_z)], axis=0)
    for d, mate in enumerate(mates):
        copy = remote(g2.at[col], g2.at[col], g2_ss.at[d], g2_rs.at[col], blk, mate)
        copy.start()
        sends.append(copy)

    total = back[reach]
    for copy, k in zip(back_copies, (1, 3, 0, 4), strict=True):
        copy.wait_recv()
        total = total + back_recv[k].astype(F32)
    gf_out[...] = jnp.transpose(total * scale_row).astype(BF16)

    for mate in mates:
        remote(g2.at[mate], g2.at[mate], g2_ss.at[0], g2_rs.at[mate], blk, mate).wait_recv()
    for c in range(COLS):
        gw_out[(c % 2) * half : (c % 2 + 1) * half, (c // 2) * fin : (c // 2 + 1) * fin] = g2[c]

    for copy in sends:
        copy.wait_send()
    loop(n_z - 1, lambda i: r2_copy(i, True).wait_send())
    loop(n_xy - 1, lambda i: r3_copy(i, True).wait_send())
    loop(n_z - 1, lambda i: g1_copy(i, True).wait_send())
    act_copy.wait()


def local(
    node_features, degree, adjacency, tile_rows, tile_cols, counts, weight, bias_vector, cotangent
):
    span = counts.shape[0]
    tile = adjacency.shape[1]
    slots = adjacency.shape[0] // span
    rows, fin = node_features.shape
    fh = weight.shape[1]
    dev_tiles = rows // tile
    n_cells = COLS * dev_tiles * dev_tiles
    n_blk = lax.axis_size("blk")
    n_z = min(ZLEN, n_blk // HI)
    n_xy = n_blk // n_z
    norm = float(rows * n_blk * COLS) ** (-0.5)

    cell = (tile_rows * dev_tiles + tile_cols).reshape(span, slots)
    index = jnp.arange(slots, dtype=jnp.int32)
    same = (cell[:, :, None] == cell[:, None, :]) & (index[None, None, :] < index[None, :, None])
    prev = jnp.max(jnp.where(same, index[None, None, :], -1), axis=2)
    prev = jnp.where(prev < 0, slots, prev).reshape(-1)
    hit = (jnp.arange(n_cells, dtype=jnp.int32)[None, :, None] == cell[:, None, :]) & (
        index[None, None, :] < counts[:, None, None]
    )
    last = jnp.max(jnp.where(hit, index[None, None, :], -1), axis=2)
    last = jnp.where(last < 0, slots, last).reshape(-1)

    half = fin // 2
    piece = half // n_z
    vmem = pltpu.VMEM
    dma = pltpu.SemaphoreType.DMA
    anywhere = pl.BlockSpec(memory_space=pl.ANY)
    in_vmem = pl.BlockSpec(memory_space=pltpu.VMEM)
    in_smem = pl.BlockSpec(memory_space=pltpu.SMEM)
    shape = jax.ShapeDtypeStruct
    act, gf, gw, gb = pl.pallas_call(
        functools.partial(kernel, n_blk, n_z, norm),
        out_shape=(
            shape((rows, fh), BF16),
            shape((rows, fin), BF16),
            shape((fin, fh), F32),
            shape((1, fh), F32),
        ),
        in_specs=[in_smem, in_smem, anywhere, in_vmem, anywhere, anywhere, in_vmem, anywhere],
        out_specs=(anywhere, in_vmem, in_vmem, in_vmem),
        scratch_shapes=[
            vmem((span, slots, tile, tile), BF16),
            vmem((slots + 1, tile, tile), F32),
            vmem((span, COLS * rows, rows), BF16),
            vmem((rows, fin), BF16),
            vmem((fin, fh), BF16),
            vmem((rows, fh), BF16),
            vmem((rows, fh), BF16),
            vmem((rows, fin), F32),
            vmem((span, rows, fin), BF16),
            vmem((rows, fin), F32),
            vmem((COLS - 1, rows, fin), BF16),
            vmem((COLS - 1, rows, fin), BF16),
            vmem((COLS, fin, rows), BF16),
            vmem((span, fin, rows), F32),
            vmem((span, fin, rows), BF16),
            vmem((span, fin, rows), BF16),
            vmem((COLS, half + 8, fin), F32),
            vmem((COLS, half + 8, fin), F32),
            vmem((n_z, piece + 8, fin), F32),
            vmem((n_z, piece + 8, fin), F32),
            vmem((n_xy, piece + 8, fin), F32),
            vmem((n_z, piece, fin), F32),
            vmem((COLS, half, fin), F32),
            dma((3,)),
            dma((span,)),
            dma,
            dma((span,)),
            dma((span,)),
            dma((COLS - 1,)),
            dma((COLS - 1,)),
            dma((COLS - 1,)),
            dma((COLS,)),
            dma((span,)),
            dma((span,)),
            dma((COLS - 1,)),
            dma((COLS,)),
            dma((n_z - 1,)),
            dma((n_z,)),
            dma((n_xy - 1,)),
            dma((n_xy,)),
            dma((n_z - 1,)),
            dma((n_z,)),
            dma((COLS - 1,)),
            dma((COLS,)),
        ],
        compiler_params=pltpu.CompilerParams(
            collective_id=0, has_side_effects=True, vmem_limit_bytes=52 * 2**20
        ),
        name="graph_layer",
    )(
        prev,
        last,
        node_features,
        degree.reshape(1, rows),
        adjacency,
        weight,
        bias_vector.reshape(1, fh),
        cotangent,
    )
    return act, gf, gw, gb.reshape(fh)


def solution(mesh):
    return jax.shard_map(
        local,
        mesh=mesh,
        in_specs=(
            P(("blk", "col"), None),
            P(("blk", "col")),
            P(("blk", "col"), None, None),
            P(("blk", "col")),
            P(("blk", "col")),
            P(("blk", "col")),
            P(),
            P(),
            P(("blk", "col"), None),
        ),
        out_specs=(P(("blk", "col"), None), P(("blk", "col"), None), P(), P()),
        check_vma=False,
    )
```

```python
import functools

import jax
import jax.numpy as jnp
from jax import lax
from jax.experimental import pallas as pl
from jax.experimental.pallas import tpu as pltpu
from jax.sharding import PartitionSpec as P

F32 = jnp.float32
BF16 = jnp.bfloat16
MESH = pl.DeviceIdType.MESH
COLS = 4
HI = 2
ZLEN = 8


def remote(src, dst, send_sem, recv_sem, blk, col):
    return pltpu.make_async_remote_copy(
        src_ref=src,
        dst_ref=dst,
        send_sem=send_sem,
        recv_sem=recv_sem,
        device_id={"blk": blk, "col": col},
        device_id_type=MESH,
    )


def loop(count, body):
    def step(i, carry):
        body(i)
        return carry

    lax.fori_loop(0, count, step, 0)


def kernel(
    n_blk,
    n_z,
    norm,
    tile_rows,
    tile_cols,
    counts,
    feats,
    deg,
    adj,
    weight,
    bias,
    cot,
    act_out,
    gf_out,
    gw_out,
    gb_out,
    tiles,
    chain,
    dense,
    feat_v,
    deg_v,
    weight_v,
    bias_v,
    cot_v,
    rows_v,
    cols_v,
    keys_v,
    index_v,
    counts_s,
    index_s,
    scale_col,
    source,
    own_sum,
    rs_send,
    rs_recv,
    hidden,
    back,
    back_send,
    back_recv,
    r1_send,
    r1_recv,
    r2_send,
    r2_recv,
    r3_recv,
    g1,
    g2,
    in_sem,
    tile_sem,
    index_sem,
    src_ss,
    src_rs,
    rs_ss,
    rs_rs,
    hid_ss,
    hid_rs,
    back_ss,
    back_rs,
    r1_ss,
    r1_rs,
    r2_ss,
    r2_rs,
    r3_ss,
    r3_rs,
    g1_ss,
    g1_rs,
    g2_ss,
    g2_rs,
):
    span, slots, tile, _ = tiles.shape
    reach = span // 2
    rows, fin = feats.shape
    dev_tiles = rows // tile
    block_tiles = COLS * dev_tiles
    n_cells = block_tiles * dev_tiles
    n_xy = n_blk // n_z
    n_x = n_xy // HI
    padded = keys_v.shape[1]

    blk = lax.axis_index("blk")
    col = lax.axis_index("col")
    hi = blk % HI
    z = (blk // HI) % n_z
    x = blk // (HI * n_z)
    xy = x * HI + hi

    def near(k):
        return (blk + k - reach + n_blk) % n_blk

    over, across, twin = (col + 2) % COLS, COLS - 1 - col, col + 1 - 2 * (col % 2)
    mates = [over, across, twin]

    def ring(step, length):
        return min(step, length - step)

    z_steps = sorted(range(1, n_z), key=lambda s: -ring(s, n_z))
    z_mates = [((z + s) % n_z, (x * n_z + (z + s) % n_z) * HI + hi) for s in z_steps]
    xy_steps = [(a, b) for a in range(n_x) for b in range(HI) if (a, b) != (0, 0)]
    xy_steps.sort(key=lambda s: -ring(s[0], n_x) - 2 * s[1])
    xy_mates = []
    for a, b in xy_steps:
        x_to, hi_to = (x + a) % n_x, (hi + b) % HI
        xy_mates.append((x_to * HI + hi_to, (x_to * n_z + z) * HI + hi_to))

    loads = [
        pltpu.make_async_copy(src, dst, in_sem.at[i])
        for i, (src, dst) in enumerate(
            (
                (deg, deg_v),
                (feats, feat_v),
                (tile_rows, rows_v),
                (tile_cols, cols_v),
                (counts, counts_s),
                (weight, weight_v),
                (bias, bias_v),
                (cot, cot_v),
            )
        )
    ]
    for load in loads[:5]:
        load.start()

    barrier = pltpu.get_barrier_semaphore()

    def hello(b, c):
        pl.semaphore_signal(barrier, inc=1, device_id={"blk": b, "col": c}, device_id_type=MESH)

    for k in (1, 3, 0, 4):
        hello(near(k), col)
    for mate in mates:
        hello(blk, mate)
    for _, other in xy_mates + z_mates:
        hello(other, col)

    def tile_copy(k):
        return pltpu.make_async_copy(adj.at[pl.ds(k * slots, slots)], tiles.at[k], tile_sem.at[k])

    loop(span, lambda k: tile_copy(k).start())

    loads[0].wait()
    scale_row = lax.rsqrt(deg_v[...].astype(F32))
    scale_col[...] = jnp.transpose(jnp.broadcast_to(scale_row, (fin, rows)))
    loads[1].wait()
    source[reach] = (scale_col[...] * feat_v[...].astype(F32)).astype(BF16)

    pl.semaphore_wait(barrier, (span - 1) + (COLS - 1) + len(xy_mates) + len(z_mates))

    sends = []
    for k in (1, 3, 0, 4):
        sends.append(
            remote(source.at[reach], source.at[k], src_ss.at[k], src_rs.at[k], near(span - 1 - k), col)
        )
        sends[-1].start()
    arrivals = list(sends)
    for load in loads[5:]:
        load.start()

    for load in loads[2:5]:
        load.wait()

    def place(lane, size):
        group = jnp.zeros_like(lane)
        for g in range(1, span):
            group += (lane >= g * size).astype(jnp.int32)
        return group

    cell = (rows_v[...] * dev_tiles + cols_v[...]).reshape(1, span * slots)
    lane = lax.broadcasted_iota(jnp.int32, cell.shape, 1)
    group = place(lane, slots)
    limit = jnp.zeros_like(lane)
    for g in range(span):
        limit = jnp.where(group == g, counts_s[g], limit)
    keys = jnp.where(lane - group * slots < limit, group * n_cells + cell, -1 - group)
    keys_v[...] = jnp.full(keys_v.shape, -1 - span, jnp.int32)
    keys_v[:, : span * slots] = keys
    key_col = jnp.transpose(jnp.broadcast_to(keys_v[...], (128, padded)))
    at = lax.broadcasted_iota(jnp.int32, key_col.shape, 0)
    for b in range(padded // 128):
        lane = lax.broadcasted_iota(jnp.int32, (1, 128), 1) + b * 128
        hit = (key_col == keys_v[:, b * 128 : (b + 1) * 128]) & (at < lane)
        found = jnp.max(jnp.where(hit, at, -1), axis=0, keepdims=True)
        index_v[:, b * 128 : (b + 1) * 128] = jnp.where(
            found < 0, slots, found - place(lane, slots) * slots
        )
        found = jnp.max(jnp.where(key_col == lane, at, -1), axis=0, keepdims=True)
        index_v[:, padded + b * 128 : padded + (b + 1) * 128] = jnp.where(
            found < 0, slots, found - place(lane, n_cells) * slots
        )
    index_copy = pltpu.make_async_copy(index_v, index_s, index_sem)
    index_copy.start()
    chain[slots] = jnp.zeros((tile, tile), F32)
    index_copy.wait()

    def build(k):
        tile_copy(k).wait()

        def slot(s):
            chain[s] = tiles[k, s].astype(F32) + chain[index_s[0, k * slots + s]]

        loop(slots, slot)

        def row(r):
            cells = [
                chain[index_s[0, padded + (k * block_tiles + r) * dev_tiles + c]].astype(BF16)
                for c in range(dev_tiles)
            ]
            dense[k, pl.ds(r * tile, tile), :] = jnp.concatenate(cells, axis=1)

        loop(block_tiles, row)

    loop(span, build)

    for copy in arrivals:
        copy.wait_recv()

    def chunk_sum(j):
        total = jnp.zeros((rows, fin), F32)
        for k in range(span):
            total += jnp.dot(
                dense[k, pl.ds(j * rows, rows), :], source[k], preferred_element_type=F32
            )
        return total

    def rs_copy(i, mate):
        copy = remote(rs_send.at[i], rs_recv.at[i], rs_ss.at[i], rs_rs.at[i], blk, mate)
        copy.start()
        sends.append(copy)
        return copy

    rs_send[0] = chunk_sum(across).astype(BF16)
    first = rs_copy(0, twin)
    partial = chunk_sum(over)
    first.wait_recv()
    rs_send[2] = (partial + rs_recv[0].astype(F32)).astype(BF16)
    third = rs_copy(2, over)
    rs_send[1] = chunk_sum(twin).astype(BF16)
    second = rs_copy(1, twin)
    own_sum[...] = chunk_sum(col)
    for load in loads[5:]:
        load.wait()
    second.wait_recv()
    own_sum[...] = own_sum[...] + rs_recv[1].astype(F32)
    third.wait_recv()
    sums = own_sum[...] + rs_recv[2].astype(F32)

    agg = scale_col[...] * sums
    agg_t = jnp.transpose(agg).astype(BF16)
    agg = agg.astype(BF16)
    pre = jnp.dot(agg, weight_v[...], preferred_element_type=F32) + bias_v[...]
    gate = jax.nn.sigmoid(pre)
    grad_pre = cot_v[...].astype(F32) * gate * (1.0 + pre * (1.0 - gate))
    low = grad_pre.astype(BF16)
    act_out[...] = (pre * gate).astype(BF16)

    part = jnp.dot(agg_t, low, preferred_element_type=F32)
    bias_part = jnp.sum(grad_pre, axis=0, keepdims=True)
    half = part.shape[0] // 2
    bias_rows = jnp.concatenate(
        [bias_part[:, :fin], bias_part[:, fin:], jnp.zeros((6, fin), F32)], axis=0
    )
    for c in range(COLS):
        r1_send[c, :half, :] = part[
            (c % 2) * half : (c % 2 + 1) * half, (c // 2) * fin : (c // 2 + 1) * fin
        ]
        r1_send[c, half:, :] = bias_rows
    r1_recv[col] = r1_send[col]
    for d, mate in enumerate(mates):
        copy = remote(r1_send.at[mate], r1_recv.at[col], r1_ss.at[d], r1_rs.at[col], blk, mate)
        copy.start()
        sends.append(copy)

    hidden_t = lax.dot_general(
        weight_v[...], low, (((1,), (1,)), ((), ())), preferred_element_type=F32
    )
    scale_row = lax.rsqrt(deg_v[...].astype(F32))
    hidden[col] = (hidden_t * scale_row).astype(BF16)

    def hidden_copy(i, c, mate):
        return remote(hidden.at[c], hidden.at[c], hid_ss.at[i], hid_rs.at[c], blk, mate)

    def hidden_send(i, c, mate):
        copy = hidden_copy(i, c, mate)
        copy.start()
        sends.append(copy)

    hidden_send(0, col, over)
    hidden_send(1, col, twin)

    def back_term(k, c):
        return jnp.dot(
            hidden[c], dense[k, pl.ds(c * rows, rows), :], preferred_element_type=F32
        )

    def back_first(k):
        back[k] = back_term(k, col)

    loop(span, back_first)

    def back_more(c):
        def one(k):
            back[k] = back[k] + back_term(k, c)

        loop(span, one)

    hidden_copy(0, twin, twin).wait_recv()
    back_more(twin)

    for mate in mates:
        remote(r1_send.at[mate], r1_recv.at[mate], r1_ss.at[0], r1_rs.at[mate], blk, mate).wait_recv()
    total = r1_recv[0] + r1_recv[1] + r1_recv[2] + r1_recv[3]
    piece = half // n_xy
    for i in range(n_xy):
        r2_send[i, :piece, :] = total[i * piece : (i + 1) * piece]
        r2_send[i, piece:, :] = total[half:]
    r2_recv[xy] = r2_send[xy]
    for i, (to, other) in enumerate(xy_mates):
        copy = remote(r2_send.at[to], r2_recv.at[xy], r2_ss.at[i], r2_rs.at[xy], other, col)
        copy.start()
        sends.append(copy)

    hidden_copy(0, over, over).wait_recv()
    hidden_send(2, over, twin)
    back_more(over)

    hidden_copy(0, across, across).wait_recv()
    back_copies = []
    for k in (1, 3, 0, 4):
        back_send[k] = (back[k] + back_term(k, across)).astype(BF16)
        copy = remote(
            back_send.at[k], back_recv.at[k], back_ss.at[k], back_rs.at[k], near(k), col
        )
        copy.start()
        back_copies.append(copy)
    sends += back_copies

    for to, other in xy_mates:
        remote(r2_send.at[to], r2_recv.at[to], r2_ss.at[0], r2_rs.at[to], other, col).wait_recv()
    total = r2_recv[0]
    for i in range(1, n_xy):
        total = total + r2_recv[i]
    r3_recv[z] = total
    for i, (to, other) in enumerate(z_mates):
        copy = remote(r3_recv.at[z], r3_recv.at[z], r3_ss.at[i], r3_rs.at[z], other, col)
        copy.start()
        sends.append(copy)

    back[reach] = back[reach] + back_term(reach, across)

    for to, other in z_mates:
        remote(r3_recv.at[to], r3_recv.at[to], r3_ss.at[0], r3_rs.at[to], other, col).wait_recv()
    total = r3_recv[0]
    for i in range(1, n_z):
        total = total + r3_recv[i]
    g1[xy] = total[:piece] * norm
    for i, (to, other) in enumerate(xy_mates):
        copy = remote(g1.at[xy], g1.at[xy], g1_ss.at[i], g1_rs.at[xy], other, col)
        copy.start()
        sends.append(copy)
    gb_out[:, :fin] = total[piece : piece + 1] * norm
    gb_out[:, fin:] = total[piece + 1 : piece + 2] * norm

    def finish_back():
        total = back[reach]
        for copy, k in zip(back_copies, (1, 3, 0, 4), strict=True):
            copy.wait_recv()
            total = total + back_recv[k].astype(F32)
        gf_out[...] = jnp.transpose(total * lax.rsqrt(deg_v[...].astype(F32))).astype(BF16)

    for to, other in xy_mates:
        remote(g1.at[to], g1.at[to], g1_ss.at[0], g1_rs.at[to], other, col).wait_recv()
    g2[col] = jnp.concatenate([g1[i] for i in range(n_xy)], axis=0)
    for d, mate in enumerate(mates):
        copy = remote(g2.at[col], g2.at[col], g2_ss.at[d], g2_rs.at[col], blk, mate)
        copy.start()
        sends.append(copy)

    finish_back()

    for mate in mates:
        remote(g2.at[mate], g2.at[mate], g2_ss.at[0], g2_rs.at[mate], blk, mate).wait_recv()
    for c in range(COLS):
        gw_out[(c % 2) * half : (c % 2 + 1) * half, (c // 2) * fin : (c // 2 + 1) * fin] = g2[c]

    for copy in sends:
        copy.wait_send()


def deliver(*refs):
    sources, results, sems = refs[:4], refs[4:8], refs[8]
    copies = [
        pltpu.make_async_copy(a, b, sems.at[i])
        for i, (a, b) in enumerate(zip(sources, results, strict=True))
    ]
    for copy in copies:
        copy.start()
    for copy in copies:
        copy.wait()


def local(
    node_features, degree, adjacency, tile_rows, tile_cols, counts, weight, bias_vector, cotangent
):
    span = counts.shape[0]
    tile = adjacency.shape[1]
    slots = adjacency.shape[0] // span
    rows, fin = node_features.shape
    fh = weight.shape[1]
    dev_tiles = rows // tile
    n_cells = COLS * dev_tiles * dev_tiles
    n_blk = lax.axis_size("blk")
    n_z = min(ZLEN, n_blk // HI)
    n_xy = n_blk // n_z
    norm = float(rows * n_blk * COLS) ** (-0.5)
    padded = -(-span * max(slots, n_cells) // 128) * 128

    half = fin // 2
    piece = half // n_xy
    vmem = pltpu.VMEM
    dma = pltpu.SemaphoreType.DMA
    anywhere = pl.BlockSpec(memory_space=pl.ANY)
    in_vmem = pl.BlockSpec(memory_space=pltpu.VMEM)
    shape = jax.ShapeDtypeStruct
    out_shape = (
        shape((rows, fh), BF16),
        shape((rows, fin), BF16),
        shape((fin, fh), F32),
        shape((1, fh), F32),
    )
    inputs = (
        tile_rows,
        tile_cols,
        counts,
        node_features,
        degree.reshape(1, rows),
        adjacency,
        weight,
        bias_vector.reshape(1, fh),
        cotangent,
    )
    results = pl.pallas_call(
        functools.partial(kernel, n_blk, n_z, norm),
        out_shape=out_shape,
        in_specs=[anywhere] * len(inputs),
        out_specs=(in_vmem,) * 4,
        scratch_shapes=[
            vmem((span, slots, tile, tile), BF16),
            vmem((slots + 1, tile, tile), F32),
            vmem((span, COLS * rows, rows), BF16),
            vmem((rows, fin), BF16),
            vmem((1, rows), jnp.int32),
            vmem((fin, fh), BF16),
            vmem((1, fh), F32),
            vmem((rows, fh), BF16),
            vmem((span * slots,), jnp.int32),
            vmem((span * slots,), jnp.int32),
            vmem((1, padded), jnp.int32),
            vmem((1, 2 * padded), jnp.int32),
            pltpu.SMEM((span,), jnp.int32),
            pltpu.SMEM((1, 2 * padded), jnp.int32),
            vmem((rows, fin), F32),
            vmem((span, rows, fin), BF16),
            vmem((rows, fin), F32),
            vmem((3, rows, fin), BF16),
            vmem((3, rows, fin), BF16),
            vmem((COLS, fin, rows), BF16),
            vmem((span, fin, rows), F32),
            vmem((span, fin, rows), BF16),
            vmem((span, fin, rows), BF16),
            vmem((COLS, half + 8, fin), F32),
            vmem((COLS, half + 8, fin), F32),
            vmem((n_xy, piece + 8, fin), F32),
            vmem((n_xy, piece + 8, fin), F32),
            vmem((n_z, piece + 8, fin), F32),
            vmem((n_xy, piece, fin), F32),
            vmem((COLS, half, fin), F32),
            dma((8,)),
            dma((span,)),
            dma,
            dma((span,)),
            dma((span,)),
            dma((3,)),
            dma((3,)),
            dma((3,)),
            dma((COLS,)),
            dma((span,)),
            dma((span,)),
            dma((3,)),
            dma((COLS,)),
            dma((n_xy - 1,)),
            dma((n_xy,)),
            dma((n_z - 1,)),
            dma((n_z,)),
            dma((n_xy - 1,)),
            dma((n_xy,)),
            dma((3,)),
            dma((COLS,)),
        ],
        compiler_params=pltpu.CompilerParams(
            collective_id=0, has_side_effects=True, vmem_limit_bytes=52 * 2**20
        ),
        name="graph_layer",
    )(*(pltpu.with_memory_space_constraint(value, pltpu.HBM) for value in inputs))
    act, gf, gw, gb = pl.pallas_call(
        deliver,
        out_shape=out_shape,
        in_specs=[anywhere] * 4,
        out_specs=(anywhere,) * 4,
        scratch_shapes=[dma((4,))],
        name="graph_results",
    )(*(pltpu.with_memory_space_constraint(value, pltpu.VMEM) for value in results))
    return act, gf, gw, gb.reshape(fh)


def solution(mesh):
    return jax.shard_map(
        local,
        mesh=mesh,
        in_specs=(
            P(("blk", "col"), None),
            P(("blk", "col")),
            P(("blk", "col"), None, None),
            P(("blk", "col")),
            P(("blk", "col")),
            P(("blk", "col")),
            P(),
            P(),
            P(("blk", "col"), None),
        ),
        out_specs=(P(("blk", "col"), None), P(("blk", "col"), None), P(), P()),
        check_vma=False,
    )
```

```python
import functools

import jax
import jax.numpy as jnp
from jax import lax
from jax.experimental import pallas as pl
from jax.experimental.pallas import tpu as pltpu
from jax.sharding import PartitionSpec as P

F32 = jnp.float32
BF16 = jnp.bfloat16
MESH = pl.DeviceIdType.MESH
COLS = 4
HI = 2
ZLEN = 8


def remote(src, dst, send_sem, recv_sem, blk, col):
    return pltpu.make_async_remote_copy(
        src_ref=src,
        dst_ref=dst,
        send_sem=send_sem,
        recv_sem=recv_sem,
        device_id={"blk": blk, "col": col},
        device_id_type=MESH,
    )


def loop(count, body):
    def step(i, carry):
        body(i)
        return carry

    lax.fori_loop(0, count, step, 0)


def kernel(
    n_blk,
    n_z,
    norm,
    tile_rows,
    tile_cols,
    counts,
    feats,
    deg,
    adj,
    weight,
    bias,
    cot,
    act_out,
    gf_out,
    gw_out,
    gb_out,
    tiles,
    chain,
    dense,
    feat_v,
    deg_v,
    weight_v,
    bias_v,
    cot_v,
    rows_v,
    cols_v,
    keys_v,
    index_v,
    counts_s,
    index_s,
    scale_col,
    source,
    own_sum,
    rs_send,
    rs_recv,
    hidden,
    back,
    back_send,
    back_recv,
    r1_send,
    r1_recv,
    r2_send,
    r2_recv,
    r3_recv,
    g2,
    in_sem,
    tile_sem,
    index_sem,
    src_ss,
    src_rs,
    rs_ss,
    rs_rs,
    hid_ss,
    hid_rs,
    back_ss,
    back_rs,
    r1_ss,
    r1_rs,
    r2_ss,
    r2_rs,
    r3_ss,
    r3_rs,
    g1_ss,
    g1_rs,
    g2_ss,
    g2_rs,
):
    span, slots, tile, _ = tiles.shape
    reach = span // 2
    rows, fin = feats.shape
    dev_tiles = rows // tile
    block_tiles = COLS * dev_tiles
    n_cells = block_tiles * dev_tiles
    n_xy = n_blk // n_z
    n_x = n_xy // HI
    padded = keys_v.shape[1]

    blk = lax.axis_index("blk")
    col = lax.axis_index("col")
    hi = blk % HI
    z = (blk // HI) % n_z
    x = blk // (HI * n_z)
    xy = x * HI + hi

    def near(k):
        return (blk + k - reach + n_blk) % n_blk

    over, across, twin = (col + 2) % COLS, COLS - 1 - col, col + 1 - 2 * (col % 2)
    mates = [over, across, twin]

    def ring(step, length):
        return min(step, length - step)

    z_steps = sorted(range(1, n_z), key=lambda s: -ring(s, n_z))
    z_mates = [((z + s) % n_z, (x * n_z + (z + s) % n_z) * HI + hi) for s in z_steps]
    xy_steps = [(a, b) for a in range(n_x) for b in range(HI) if (a, b) != (0, 0)]
    xy_steps.sort(key=lambda s: -ring(s[0], n_x) - 2 * s[1])
    xy_mates = []
    for a, b in xy_steps:
        x_to, hi_to = (x + a) % n_x, (hi + b) % HI
        xy_mates.append((x_to * HI + hi_to, (x_to * n_z + z) * HI + hi_to))
    plane = [(c, to, other) for to, other in xy_mates for c in (col, over)] + [(over, xy, blk)]

    loads = [
        pltpu.make_async_copy(src, dst, in_sem.at[i])
        for i, (src, dst) in enumerate(
            (
                (deg, deg_v),
                (feats, feat_v),
                (tile_rows, rows_v),
                (tile_cols, cols_v),
                (counts, counts_s),
                (weight, weight_v),
                (bias, bias_v),
                (cot, cot_v),
            )
        )
    ]
    for load in loads[:5]:
        load.start()

    barrier = pltpu.get_barrier_semaphore()

    def hello(b, c):
        pl.semaphore_signal(barrier, inc=1, device_id={"blk": b, "col": c}, device_id_type=MESH)

    for k in (1, 3, 0, 4):
        hello(near(k), col)
    for mate in mates:
        hello(blk, mate)
    for _, other in xy_mates:
        hello(other, col)
        hello(other, over)
    for _, other in z_mates:
        hello(other, col)

    def tile_copy(k):
        return pltpu.make_async_copy(adj.at[pl.ds(k * slots, slots)], tiles.at[k], tile_sem.at[k])

    loop(span, lambda k: tile_copy(k).start())

    loads[0].wait()
    scale_row = lax.rsqrt(deg_v[...].astype(F32))
    scale_col[...] = jnp.transpose(jnp.broadcast_to(scale_row, (fin, rows)))
    loads[1].wait()
    source[reach] = (scale_col[...] * feat_v[...].astype(F32)).astype(BF16)

    pl.semaphore_wait(barrier, (span - 1) + (COLS - 1) + 2 * len(xy_mates) + len(z_mates))

    sends = []
    for k in (1, 3, 0, 4):
        sends.append(
            remote(source.at[reach], source.at[k], src_ss.at[k], src_rs.at[k], near(span - 1 - k), col)
        )
        sends[-1].start()
    arrivals = list(sends)
    for load in loads[5:]:
        load.start()

    for load in loads[2:5]:
        load.wait()

    def place(lane, size):
        group = jnp.zeros_like(lane)
        for g in range(1, span):
            group += (lane >= g * size).astype(jnp.int32)
        return group

    cell = (rows_v[...] * dev_tiles + cols_v[...]).reshape(1, span * slots)
    lane = lax.broadcasted_iota(jnp.int32, cell.shape, 1)
    group = place(lane, slots)
    limit = jnp.zeros_like(lane)
    for g in range(span):
        limit = jnp.where(group == g, counts_s[g], limit)
    keys = jnp.where(lane - group * slots < limit, group * n_cells + cell, -1 - group)
    keys_v[...] = jnp.full(keys_v.shape, -1 - span, jnp.int32)
    keys_v[:, : span * slots] = keys
    key_col = jnp.transpose(jnp.broadcast_to(keys_v[...], (128, padded)))
    at = lax.broadcasted_iota(jnp.int32, key_col.shape, 0)
    for b in range(padded // 128):
        lane = lax.broadcasted_iota(jnp.int32, (1, 128), 1) + b * 128
        hit = (key_col == keys_v[:, b * 128 : (b + 1) * 128]) & (at < lane)
        found = jnp.max(jnp.where(hit, at, -1), axis=0, keepdims=True)
        index_v[:, b * 128 : (b + 1) * 128] = jnp.where(
            found < 0, slots, found - place(lane, slots) * slots
        )
        found = jnp.max(jnp.where(key_col == lane, at, -1), axis=0, keepdims=True)
        index_v[:, padded + b * 128 : padded + (b + 1) * 128] = jnp.where(
            found < 0, slots, found - place(lane, n_cells) * slots
        )
    index_copy = pltpu.make_async_copy(index_v, index_s, index_sem)
    index_copy.start()
    chain[slots] = jnp.zeros((tile, tile), F32)
    index_copy.wait()

    def build(k):
        tile_copy(k).wait()

        def slot(s):
            chain[s] = tiles[k, s].astype(F32) + chain[index_s[0, k * slots + s]]

        loop(slots, slot)

        def row(r):
            cells = [
                chain[index_s[0, padded + (k * block_tiles + r) * dev_tiles + c]].astype(BF16)
                for c in range(dev_tiles)
            ]
            dense[k, pl.ds(r * tile, tile), :] = jnp.concatenate(cells, axis=1)

        loop(block_tiles, row)

    loop(span, build)

    for copy in arrivals:
        copy.wait_recv()

    side = rows // 2

    def chunk_sum(j, h):
        total = jnp.zeros((side, fin), F32)
        for k in range(span):
            total += jnp.dot(
                dense[k, pl.ds(j * rows + h * side, side), :],
                source[k],
                preferred_element_type=F32,
            )
        return total

    def rs_copy(i, h, mate):
        copy = remote(rs_send.at[i, h], rs_recv.at[i, h], rs_ss.at[i, h], rs_rs.at[i, h], blk, mate)
        copy.start()
        sends.append(copy)
        return copy

    first, second, third = [], [], []
    for h in range(2):
        rs_send[0, h] = chunk_sum(across, h).astype(BF16)
        first.append(rs_copy(0, h, twin))
    for h in range(2):
        partial = chunk_sum(over, h)
        first[h].wait_recv()
        rs_send[2, h] = (partial + rs_recv[0, h].astype(F32)).astype(BF16)
        third.append(rs_copy(2, h, over))
    for h in range(2):
        rs_send[1, h] = chunk_sum(twin, h).astype(BF16)
        second.append(rs_copy(1, h, twin))
    for h in range(2):
        own_sum[h] = chunk_sum(col, h)
    for load in loads[5:]:
        load.wait()
    for h in range(2):
        second[h].wait_recv()
        own_sum[h] = own_sum[h] + rs_recv[1, h].astype(F32)

    def hidden_copy(i, c, h, mate):
        return remote(
            hidden.at[c, h], hidden.at[c, h], hid_ss.at[i, h], hid_rs.at[c, h], blk, mate
        )

    def hidden_send(i, c, h, mate):
        copy = hidden_copy(i, c, h, mate)
        copy.start()
        sends.append(copy)

    part = jnp.zeros((fin, weight_v.shape[1]), F32)
    bias_part = jnp.zeros((1, weight_v.shape[1]), F32)
    for h in range(2):
        third[h].wait_recv()
        sums = own_sum[h] + rs_recv[2, h].astype(F32)
        agg = scale_col[h * side : (h + 1) * side] * sums
        agg_t = jnp.transpose(agg).astype(BF16)
        agg = agg.astype(BF16)
        pre = jnp.dot(agg, weight_v[...], preferred_element_type=F32) + bias_v[...]
        gate = jax.nn.sigmoid(pre)
        cot_h = cot_v[h * side : (h + 1) * side].astype(F32)
        grad_pre = cot_h * gate * (1.0 + pre * (1.0 - gate))
        low = grad_pre.astype(BF16)
        hidden_t = lax.dot_general(
            weight_v[...], low, (((1,), (1,)), ((), ())), preferred_element_type=F32
        )
        scale_row = lax.rsqrt(deg_v[:, h * side : (h + 1) * side].astype(F32))
        hidden[col, h] = (hidden_t * scale_row).astype(BF16)
        hidden_send(0, col, h, over)
        hidden_send(1, col, h, twin)
        act_out[h * side : (h + 1) * side] = (pre * gate).astype(BF16)
        part += jnp.dot(agg_t, low, preferred_element_type=F32)
        bias_part += jnp.sum(grad_pre, axis=0, keepdims=True)

    half = part.shape[0] // 2
    bias_rows = jnp.concatenate(
        [bias_part[:, :fin], bias_part[:, fin:], jnp.zeros((6, fin), F32)], axis=0
    )
    for c in range(COLS):
        r1_send[c, :half, :] = part[
            (c % 2) * half : (c % 2 + 1) * half, (c // 2) * fin : (c // 2 + 1) * fin
        ]
        r1_send[c, half:, :] = bias_rows
    for i, c in enumerate((across, twin)):
        copy = remote(r1_send.at[c], r1_recv.at[c], r1_ss.at[i], r1_rs.at[c // 2], blk, twin)
        copy.start()
        sends.append(copy)

    def back_term(k, c):
        total = jnp.zeros((fin, rows), F32)
        for h in range(2):
            total += jnp.dot(
                hidden[c, h],
                dense[k, pl.ds(c * rows + h * side, side), :],
                preferred_element_type=F32,
            )
        return total

    def back_more(c):
        def one(k):
            back[k] = back[k] + back_term(k, c)

        loop(span, one)

    core = col % 2
    piece = half // n_xy
    for lo in range(2):
        c = 2 * lo + core
        remote(r1_send.at[c], r1_recv.at[c], r1_ss.at[0], r1_rs.at[lo], blk, twin).wait_recv()
        total = r1_send[c] + r1_recv[c]
        for i in range(n_xy):
            r2_send[lo, i, :piece, :] = total[i * piece : (i + 1) * piece]
            r2_send[lo, i, piece:, :] = total[half:]
    r2_recv[col // 2, xy] = r2_send[col // 2, xy]
    for i, (c, to, other) in enumerate(plane):
        copy = remote(
            r2_send.at[c // 2, to],
            r2_recv.at[col // 2, xy],
            r2_ss.at[i],
            r2_rs.at[col // 2, xy],
            other,
            c,
        )
        copy.start()
        sends.append(copy)

    def back_first(k):
        back[k] = back_term(k, col)

    loop(span, back_first)

    for h in range(2):
        hidden_copy(0, over, h, over).wait_recv()
        hidden_send(2, over, h, twin)
    for h in range(2):
        hidden_copy(0, twin, h, twin).wait_recv()
    back_more(twin)
    back_more(over)

    for c, to, other in plane:
        remote(
            r2_send.at[c // 2, to],
            r2_recv.at[c // 2, to],
            r2_ss.at[0],
            r2_rs.at[c // 2, to],
            other,
            c,
        ).wait_recv()
    total = jnp.zeros((piece + 8, fin), F32)
    for lo in range(2):
        for i in range(n_xy):
            total = total + r2_recv[lo, i]
    r3_recv[z] = total
    for i, (to, other) in enumerate(z_mates):
        copy = remote(r3_recv.at[z], r3_recv.at[z], r3_ss.at[i], r3_rs.at[z], other, col)
        copy.start()
        sends.append(copy)

    for h in range(2):
        hidden_copy(0, across, h, across).wait_recv()
    back_copies = []
    for k in (1, 3, 0, 4):
        back_send[k] = (back[k] + back_term(k, across)).astype(BF16)
        copy = remote(
            back_send.at[k], back_recv.at[k], back_ss.at[k], back_rs.at[k], near(k), col
        )
        copy.start()
        back_copies.append(copy)
    sends += back_copies

    back[reach] = back[reach] + back_term(reach, across)

    for to, other in z_mates:
        remote(r3_recv.at[to], r3_recv.at[to], r3_ss.at[0], r3_rs.at[to], other, col).wait_recv()
    total = r3_recv[0]
    for i in range(1, n_z):
        total = total + r3_recv[i]
    g2[col, xy] = total[:piece] * norm
    for i, (c, to, other) in enumerate(plane):
        copy = remote(g2.at[col, xy], g2.at[col, xy], g1_ss.at[i], g1_rs.at[col // 2, xy], other, c)
        copy.start()
        sends.append(copy)
    gb_out[:, :fin] = total[piece : piece + 1] * norm
    gb_out[:, fin:] = total[piece + 1 : piece + 2] * norm

    def finish_back():
        total = back[reach]
        for copy, k in zip(back_copies, (1, 3, 0, 4), strict=True):
            copy.wait_recv()
            total = total + back_recv[k].astype(F32)
        gf_out[...] = jnp.transpose(total * lax.rsqrt(deg_v[...].astype(F32))).astype(BF16)

    for c, to, other in plane:
        remote(g2.at[c, to], g2.at[c, to], g1_ss.at[0], g1_rs.at[c // 2, to], other, c).wait_recv()
    for i, c in enumerate((col, over)):
        copy = remote(g2.at[c], g2.at[c], g2_ss.at[i], g2_rs.at[c // 2], blk, twin)
        copy.start()
        sends.append(copy)
    finish_back()
    for c in (twin, across):
        remote(g2.at[c], g2.at[c], g2_ss.at[0], g2_rs.at[c // 2], blk, twin).wait_recv()
    for c in range(COLS):
        for i in range(n_xy):
            top = (c % 2) * half + i * piece
            gw_out[top : top + piece, (c // 2) * fin : (c // 2 + 1) * fin] = g2[c, i]

    for copy in sends:
        copy.wait_send()


def deliver(*refs):
    sources, results, sems = refs[:4], refs[4:8], refs[8]
    copies = [
        pltpu.make_async_copy(a, b, sems.at[i])
        for i, (a, b) in enumerate(zip(sources, results, strict=True))
    ]
    for copy in copies:
        copy.start()
    for copy in copies:
        copy.wait()


def local(
    node_features, degree, adjacency, tile_rows, tile_cols, counts, weight, bias_vector, cotangent
):
    span = counts.shape[0]
    tile = adjacency.shape[1]
    slots = adjacency.shape[0] // span
    rows, fin = node_features.shape
    fh = weight.shape[1]
    dev_tiles = rows // tile
    n_cells = COLS * dev_tiles * dev_tiles
    n_blk = lax.axis_size("blk")
    n_z = min(ZLEN, n_blk // HI)
    n_xy = n_blk // n_z
    norm = float(rows * n_blk * COLS) ** (-0.5)
    padded = -(-span * max(slots, n_cells) // 128) * 128

    half = fin // 2
    piece = half // n_xy
    vmem = pltpu.VMEM
    dma = pltpu.SemaphoreType.DMA
    anywhere = pl.BlockSpec(memory_space=pl.ANY)
    in_vmem = pl.BlockSpec(memory_space=pltpu.VMEM)
    shape = jax.ShapeDtypeStruct
    out_shape = (
        shape((rows, fh), BF16),
        shape((rows, fin), BF16),
        shape((fin, fh), F32),
        shape((1, fh), F32),
    )
    inputs = (
        tile_rows,
        tile_cols,
        counts,
        node_features,
        degree.reshape(1, rows),
        adjacency,
        weight,
        bias_vector.reshape(1, fh),
        cotangent,
    )
    results = pl.pallas_call(
        functools.partial(kernel, n_blk, n_z, norm),
        out_shape=out_shape,
        in_specs=[anywhere] * len(inputs),
        out_specs=(in_vmem,) * 4,
        scratch_shapes=[
            vmem((span, slots, tile, tile), BF16),
            vmem((slots + 1, tile, tile), F32),
            vmem((span, COLS * rows, rows), BF16),
            vmem((rows, fin), BF16),
            vmem((1, rows), jnp.int32),
            vmem((fin, fh), BF16),
            vmem((1, fh), F32),
            vmem((rows, fh), BF16),
            vmem((span * slots,), jnp.int32),
            vmem((span * slots,), jnp.int32),
            vmem((1, padded), jnp.int32),
            vmem((1, 2 * padded), jnp.int32),
            pltpu.SMEM((span,), jnp.int32),
            pltpu.SMEM((1, 2 * padded), jnp.int32),
            vmem((rows, fin), F32),
            vmem((span, rows, fin), BF16),
            vmem((2, rows // 2, fin), F32),
            vmem((3, 2, rows // 2, fin), BF16),
            vmem((3, 2, rows // 2, fin), BF16),
            vmem((COLS, 2, fin, rows // 2), BF16),
            vmem((span, fin, rows), F32),
            vmem((span, fin, rows), BF16),
            vmem((span, fin, rows), BF16),
            vmem((COLS, half + 8, fin), F32),
            vmem((COLS, half + 8, fin), F32),
            vmem((2, n_xy, piece + 8, fin), F32),
            vmem((2, n_xy, piece + 8, fin), F32),
            vmem((n_z, piece + 8, fin), F32),
            vmem((COLS, n_xy, piece, fin), F32),
            dma((8,)),
            dma((span,)),
            dma,
            dma((span,)),
            dma((span,)),
            dma((3, 2)),
            dma((3, 2)),
            dma((3, 2)),
            dma((COLS, 2)),
            dma((span,)),
            dma((span,)),
            dma((2,)),
            dma((2,)),
            dma((2 * n_xy - 1,)),
            dma((2, n_xy)),
            dma((n_z - 1,)),
            dma((n_z,)),
            dma((2 * n_xy - 1,)),
            dma((2, n_xy)),
            dma((2,)),
            dma((2,)),
        ],
        compiler_params=pltpu.CompilerParams(
            collective_id=0, has_side_effects=True, vmem_limit_bytes=52 * 2**20
        ),
        name="graph_layer",
    )(*(pltpu.with_memory_space_constraint(value, pltpu.HBM) for value in inputs))
    act, gf, gw, gb = pl.pallas_call(
        deliver,
        out_shape=out_shape,
        in_specs=[anywhere] * 4,
        out_specs=(anywhere,) * 4,
        scratch_shapes=[dma((4,))],
        name="graph_results",
    )(*(pltpu.with_memory_space_constraint(value, pltpu.VMEM) for value in results))
    return act, gf, gw, gb.reshape(fh)


def solution(mesh):
    return jax.shard_map(
        local,
        mesh=mesh,
        in_specs=(
            P(("blk", "col"), None),
            P(("blk", "col")),
            P(("blk", "col"), None, None),
            P(("blk", "col")),
            P(("blk", "col")),
            P(("blk", "col")),
            P(),
            P(),
            P(("blk", "col"), None),
        ),
        out_specs=(P(("blk", "col"), None), P(("blk", "col"), None), P(), P()),
        check_vma=False,
    )
```

```python
import functools

import jax
import jax.numpy as jnp
from jax import lax
from jax.experimental import pallas as pl
from jax.experimental.pallas import tpu as pltpu
from jax.sharding import PartitionSpec as P

F32 = jnp.float32
BF16 = jnp.bfloat16
MESH = pl.DeviceIdType.MESH
COLS = 4
HI = 2
ZLEN = 8
WAYS = 3


def remote(src, dst, send_sem, recv_sem, blk, col):
    return pltpu.make_async_remote_copy(
        src_ref=src,
        dst_ref=dst,
        send_sem=send_sem,
        recv_sem=recv_sem,
        device_id={"blk": blk, "col": col},
        device_id_type=MESH,
    )


def loop(count, body):
    def step(i, carry):
        body(i)
        return carry

    lax.fori_loop(0, count, step, 0)


def kernel(
    n_blk,
    n_z,
    norm,
    tile_rows,
    tile_cols,
    counts,
    feats,
    deg,
    adj,
    weight,
    bias,
    cot,
    act_out,
    gf_out,
    gw_out,
    gb_out,
    tiles,
    chain,
    dense,
    feat_v,
    deg_v,
    weight_v,
    bias_v,
    cot_v,
    rows_v,
    cols_v,
    keys_v,
    index_v,
    counts_s,
    index_s,
    scale_col,
    source,
    own_sum,
    rs_send,
    rs_recv,
    hidden,
    back,
    back_send,
    back_recv,
    r1_send,
    r1_recv,
    r2_send,
    r2_recv,
    r3_recv,
    g2,
    in_sem,
    tile_sem,
    index_sem,
    src_ss,
    src_rs,
    rs_ss,
    rs_rs,
    hid_ss,
    hid_rs,
    back_ss,
    back_rs,
    r1_ss,
    r1_rs,
    r2_ss,
    r2_rs,
    r3_ss,
    r3_rs,
    g1_ss,
    g1_rs,
    g2_ss,
    g2_rs,
):
    span, slots, tile, _ = tiles.shape
    reach = span // 2
    rows, fin = feats.shape
    dev_tiles = rows // tile
    block_tiles = COLS * dev_tiles
    n_cells = block_tiles * dev_tiles
    n_xy = n_blk // n_z
    n_x = n_xy // HI
    padded = keys_v.shape[1]

    blk = lax.axis_index("blk")
    col = lax.axis_index("col")
    hi = blk % HI
    z = (blk // HI) % n_z
    x = blk // (HI * n_z)
    xy = x * HI + hi

    def near(k):
        return (blk + k - reach + n_blk) % n_blk

    over, across, twin = (col + 2) % COLS, COLS - 1 - col, col + 1 - 2 * (col % 2)
    mates = [over, across, twin]

    def ring(step, length):
        return min(step, length - step)

    z_steps = sorted(range(1, n_z), key=lambda s: -ring(s, n_z))
    z_mates = [((z + s) % n_z, (x * n_z + (z + s) % n_z) * HI + hi) for s in z_steps]
    xy_steps = [(a, b) for a in range(n_x) for b in range(HI) if (a, b) != (0, 0)]
    xy_steps.sort(key=lambda s: -ring(s[0], n_x) - 2 * s[1])
    xy_mates = []
    for a, b in xy_steps:
        x_to, hi_to = (x + a) % n_x, (hi + b) % HI
        xy_mates.append((x_to * HI + hi_to, (x_to * n_z + z) * HI + hi_to))
    plane = [(c, to, other) for to, other in xy_mates for c in (col, over)] + [(over, xy, blk)]

    loads = [
        pltpu.make_async_copy(src, dst, in_sem.at[i])
        for i, (src, dst) in enumerate(
            (
                (deg, deg_v),
                (feats, feat_v),
                (tile_rows, rows_v),
                (tile_cols, cols_v),
                (counts, counts_s),
                (weight, weight_v),
                (bias, bias_v),
                (cot, cot_v),
            )
        )
    ]
    for load in loads[:5]:
        load.start()

    barrier = pltpu.get_barrier_semaphore()

    def hello(b, c):
        pl.semaphore_signal(barrier, inc=1, device_id={"blk": b, "col": c}, device_id_type=MESH)

    for k in (1, 3, 0, 4):
        hello(near(k), col)
    for mate in mates:
        hello(blk, mate)
    for _, other in xy_mates:
        hello(other, col)
        hello(other, over)
    for _, other in z_mates:
        hello(other, col)

    def tile_copy(k):
        return pltpu.make_async_copy(adj.at[pl.ds(k * slots, slots)], tiles.at[k], tile_sem.at[k])

    loop(span, lambda k: tile_copy(k).start())

    loads[0].wait()
    scale_row = lax.rsqrt(deg_v[...].astype(F32))
    scale_col[...] = jnp.transpose(jnp.broadcast_to(scale_row, (fin, rows)))
    loads[1].wait()
    source[reach] = (scale_col[...] * feat_v[...].astype(F32)).astype(BF16)

    pl.semaphore_wait(barrier, (span - 1) + (COLS - 1) + 2 * len(xy_mates) + len(z_mates))

    sends = []
    for k in (1, 3, 0, 4):
        sends.append(
            remote(source.at[reach], source.at[k], src_ss.at[k], src_rs.at[k], near(span - 1 - k), col)
        )
        sends[-1].start()
    arrivals = list(sends)
    for load in loads[5:]:
        load.start()

    for load in loads[2:5]:
        load.wait()

    def place(lane, size):
        group = jnp.zeros_like(lane)
        for g in range(1, span):
            group += (lane >= g * size).astype(jnp.int32)
        return group

    cell = (rows_v[...] * dev_tiles + cols_v[...]).reshape(1, span * slots)
    lane = lax.broadcasted_iota(jnp.int32, cell.shape, 1)
    group = place(lane, slots)
    limit = jnp.zeros_like(lane)
    for g in range(span):
        limit = jnp.where(group == g, counts_s[g], limit)
    keys = jnp.where(lane - group * slots < limit, group * n_cells + cell, -1 - group)
    keys_v[...] = jnp.full(keys_v.shape, -1 - span, jnp.int32)
    keys_v[:, : span * slots] = keys
    key_col = jnp.transpose(jnp.broadcast_to(keys_v[...], (128, padded)))
    at = lax.broadcasted_iota(jnp.int32, key_col.shape, 0)
    for b in range(padded // 128):
        lane = lax.broadcasted_iota(jnp.int32, (1, 128), 1) + b * 128
        hit = (key_col == keys_v[:, b * 128 : (b + 1) * 128]) & (at < lane)
        found = jnp.max(jnp.where(hit, at, -1), axis=0, keepdims=True)
        index_v[:, b * 128 : (b + 1) * 128] = jnp.where(
            found < 0, slots, found - place(lane, slots) * slots
        )
        found = jnp.max(jnp.where(key_col == lane, at, -1), axis=0, keepdims=True)
        index_v[:, padded + b * 128 : padded + (b + 1) * 128] = jnp.where(
            found < 0, slots, found - place(lane, n_cells) * slots
        )
    index_copy = pltpu.make_async_copy(index_v, index_s, index_sem)
    index_copy.start()
    for i in range(WAYS):
        chain[i, slots] = jnp.zeros((tile, tile), F32)
    index_copy.wait()

    def build(offsets):
        for k in offsets:
            tile_copy(k).wait()

        def slot(s):
            values = [
                tiles[k, s].astype(F32) + chain[i, index_s[0, k * slots + s]]
                for i, k in enumerate(offsets)
            ]
            for i, value in enumerate(values):
                chain[i, s] = value

        loop(slots, slot)

        def row(r):
            for i, k in enumerate(offsets):
                cells = [
                    chain[i, index_s[0, padded + (k * block_tiles + r) * dev_tiles + c]].astype(BF16)
                    for c in range(dev_tiles)
                ]
                dense[k, pl.ds(r * tile, tile), :] = jnp.concatenate(cells, axis=1)

        loop(block_tiles, row)

    for first in range(0, span, WAYS):
        build(range(first, min(first + WAYS, span)))

    for copy in arrivals:
        copy.wait_recv()

    side = rows // 2

    def chunk_sum(j, h):
        total = jnp.zeros((side, fin), F32)
        for k in range(span):
            total += jnp.dot(
                dense[k, pl.ds(j * rows + h * side, side), :],
                source[k],
                preferred_element_type=F32,
            )
        return total

    def rs_copy(i, h, mate):
        copy = remote(rs_send.at[i, h], rs_recv.at[i, h], rs_ss.at[i, h], rs_rs.at[i, h], blk, mate)
        copy.start()
        sends.append(copy)
        return copy

    first, second, third = [], [], []
    for h in range(2):
        rs_send[0, h] = chunk_sum(across, h).astype(BF16)
        first.append(rs_copy(0, h, twin))
    for h in range(2):
        partial = chunk_sum(over, h)
        first[h].wait_recv()
        rs_send[2, h] = (partial + rs_recv[0, h].astype(F32)).astype(BF16)
        third.append(rs_copy(2, h, over))
    for h in range(2):
        rs_send[1, h] = chunk_sum(twin, h).astype(BF16)
        second.append(rs_copy(1, h, twin))
    for h in range(2):
        own_sum[h] = chunk_sum(col, h)
    for load in loads[5:]:
        load.wait()
    for h in range(2):
        second[h].wait_recv()
        own_sum[h] = own_sum[h] + rs_recv[1, h].astype(F32)

    def hidden_copy(i, c, h, mate):
        return remote(
            hidden.at[c, h], hidden.at[c, h], hid_ss.at[i, h], hid_rs.at[c, h], blk, mate
        )

    def hidden_send(i, c, h, mate):
        copy = hidden_copy(i, c, h, mate)
        copy.start()
        sends.append(copy)

    part = jnp.zeros((fin, weight_v.shape[1]), F32)
    bias_part = jnp.zeros((1, weight_v.shape[1]), F32)
    for h in range(2):
        third[h].wait_recv()
        sums = own_sum[h] + rs_recv[2, h].astype(F32)
        agg = scale_col[h * side : (h + 1) * side] * sums
        agg_t = jnp.transpose(agg).astype(BF16)
        agg = agg.astype(BF16)
        pre = jnp.dot(agg, weight_v[...], preferred_element_type=F32) + bias_v[...]
        gate = jax.nn.sigmoid(pre)
        cot_h = cot_v[h * side : (h + 1) * side].astype(F32)
        grad_pre = cot_h * gate * (1.0 + pre * (1.0 - gate))
        low = grad_pre.astype(BF16)
        hidden_t = lax.dot_general(
            weight_v[...], low, (((1,), (1,)), ((), ())), preferred_element_type=F32
        )
        scale_row = lax.rsqrt(deg_v[:, h * side : (h + 1) * side].astype(F32))
        hidden[col, h] = (hidden_t * scale_row).astype(BF16)
        hidden_send(0, col, h, over)
        act_out[h * side : (h + 1) * side] = (pre * gate).astype(BF16)
        part += jnp.dot(agg_t, low, preferred_element_type=F32)
        bias_part += jnp.sum(grad_pre, axis=0, keepdims=True)

    copy = remote(hidden.at[col], hidden.at[col], hid_ss.at[1, 0], hid_rs.at[col, 0], blk, twin)
    copy.start()
    sends.append(copy)

    half = part.shape[0] // 2
    bias_rows = jnp.concatenate(
        [bias_part[:, :fin], bias_part[:, fin:], jnp.zeros((6, fin), F32)], axis=0
    )
    for c in range(COLS):
        r1_send[c, :half, :] = part[
            (c % 2) * half : (c % 2 + 1) * half, (c // 2) * fin : (c // 2 + 1) * fin
        ]
        r1_send[c, half:, :] = bias_rows
    for i, c in enumerate((across, twin)):
        copy = remote(r1_send.at[c], r1_recv.at[c], r1_ss.at[i], r1_rs.at[c // 2], blk, twin)
        copy.start()
        sends.append(copy)

    def back_term(k, c):
        total = jnp.zeros((fin, rows), F32)
        for h in range(2):
            total += jnp.dot(
                hidden[c, h],
                dense[k, pl.ds(c * rows + h * side, side), :],
                preferred_element_type=F32,
            )
        return total

    def back_more(c):
        def one(k):
            back[k] = back[k] + back_term(k, c)

        loop(span, one)

    core = col % 2
    piece = half // n_xy
    used = pl.ds(0, piece + 2)
    for lo in range(2):
        c = 2 * lo + core
        remote(r1_send.at[c], r1_recv.at[c], r1_ss.at[0], r1_rs.at[lo], blk, twin).wait_recv()
        total = r1_send[c] + r1_recv[c]
        for i in range(n_xy):
            r2_send[lo, i, :piece, :] = total[i * piece : (i + 1) * piece]
            r2_send[lo, i, piece:, :] = total[half:]
    r2_recv[col // 2, xy] = r2_send[col // 2, xy]
    for i, (c, to, other) in enumerate(plane):
        copy = remote(
            r2_send.at[c // 2, to, used],
            r2_recv.at[col // 2, xy, used],
            r2_ss.at[i],
            r2_rs.at[col // 2, xy],
            other,
            c,
        )
        copy.start()
        sends.append(copy)

    def back_first(k):
        back[k] = back_term(k, col)

    loop(span, back_first)

    for h in range(2):
        hidden_copy(0, over, h, over).wait_recv()
        hidden_send(2, over, h, twin)
    remote(hidden.at[twin], hidden.at[twin], hid_ss.at[0, 0], hid_rs.at[twin, 0], blk, twin).wait_recv()
    back_more(twin)
    back_more(over)

    for c, to, other in plane:
        remote(
            r2_send.at[c // 2, to, used],
            r2_recv.at[c // 2, to, used],
            r2_ss.at[0],
            r2_rs.at[c // 2, to],
            other,
            c,
        ).wait_recv()
    total = jnp.zeros((piece + 2, fin), F32)
    for lo in range(2):
        for i in range(n_xy):
            total = total + r2_recv[lo, i, used]
    r3_recv[z, used] = total
    for i, (to, other) in enumerate(z_mates):
        copy = remote(r3_recv.at[z, used], r3_recv.at[z, used], r3_ss.at[i], r3_rs.at[z], other, col)
        copy.start()
        sends.append(copy)

    for h in range(2):
        hidden_copy(0, across, h, across).wait_recv()
    back_copies = []
    for k in (1, 3, 0, 4):
        back_send[k] = (back[k] + back_term(k, across)).astype(BF16)
        copy = remote(
            back_send.at[k], back_recv.at[k], back_ss.at[k], back_rs.at[k], near(k), col
        )
        copy.start()
        back_copies.append(copy)
    sends += back_copies

    back[reach] = back[reach] + back_term(reach, across)

    for to, other in z_mates:
        remote(
            r3_recv.at[to, used], r3_recv.at[to, used], r3_ss.at[0], r3_rs.at[to], other, col
        ).wait_recv()
    total = r3_recv[0, used]
    for i in range(1, n_z):
        total = total + r3_recv[i, used]
    g2[col, xy] = total[:piece] * norm
    for i, (c, to, other) in enumerate(plane):
        copy = remote(g2.at[col, xy], g2.at[col, xy], g1_ss.at[i], g1_rs.at[col // 2, xy], other, c)
        copy.start()
        sends.append(copy)
    gb_out[:, :fin] = total[piece : piece + 1] * norm
    gb_out[:, fin:] = total[piece + 1 : piece + 2] * norm

    def finish_back():
        total = back[reach]
        for copy, k in zip(back_copies, (1, 3, 0, 4), strict=True):
            copy.wait_recv()
            total = total + back_recv[k].astype(F32)
        gf_out[...] = jnp.transpose(total * lax.rsqrt(deg_v[...].astype(F32))).astype(BF16)

    for c, to, other in plane:
        remote(g2.at[c, to], g2.at[c, to], g1_ss.at[0], g1_rs.at[c // 2, to], other, c).wait_recv()
    for i, c in enumerate((col, over)):
        copy = remote(g2.at[c], g2.at[c], g2_ss.at[i], g2_rs.at[c // 2], blk, twin)
        copy.start()
        sends.append(copy)
    finish_back()
    for c in (twin, across):
        remote(g2.at[c], g2.at[c], g2_ss.at[0], g2_rs.at[c // 2], blk, twin).wait_recv()
    for c in range(COLS):
        for i in range(n_xy):
            top = (c % 2) * half + i * piece
            gw_out[top : top + piece, (c // 2) * fin : (c // 2 + 1) * fin] = g2[c, i]

    for copy in sends:
        copy.wait_send()


def deliver(*refs):
    sources, results, sems = refs[:4], refs[4:8], refs[8]
    copies = [
        pltpu.make_async_copy(a, b, sems.at[i])
        for i, (a, b) in enumerate(zip(sources, results, strict=True))
    ]
    for copy in copies:
        copy.start()
    for copy in copies:
        copy.wait()


def local(
    node_features, degree, adjacency, tile_rows, tile_cols, counts, weight, bias_vector, cotangent
):
    span = counts.shape[0]
    tile = adjacency.shape[1]
    slots = adjacency.shape[0] // span
    rows, fin = node_features.shape
    fh = weight.shape[1]
    dev_tiles = rows // tile
    n_cells = COLS * dev_tiles * dev_tiles
    n_blk = lax.axis_size("blk")
    n_z = min(ZLEN, n_blk // HI)
    n_xy = n_blk // n_z
    norm = float(rows * n_blk * COLS) ** (-0.5)
    padded = -(-span * max(slots, n_cells) // 128) * 128

    half = fin // 2
    piece = half // n_xy
    vmem = pltpu.VMEM
    dma = pltpu.SemaphoreType.DMA
    anywhere = pl.BlockSpec(memory_space=pl.ANY)
    in_vmem = pl.BlockSpec(memory_space=pltpu.VMEM)
    shape = jax.ShapeDtypeStruct
    out_shape = (
        shape((rows, fh), BF16),
        shape((rows, fin), BF16),
        shape((fin, fh), F32),
        shape((1, fh), F32),
    )
    inputs = (
        tile_rows,
        tile_cols,
        counts,
        node_features,
        degree.reshape(1, rows),
        adjacency,
        weight,
        bias_vector.reshape(1, fh),
        cotangent,
    )
    results = pl.pallas_call(
        functools.partial(kernel, n_blk, n_z, norm),
        out_shape=out_shape,
        in_specs=[anywhere] * len(inputs),
        out_specs=(in_vmem,) * 4,
        scratch_shapes=[
            vmem((span, slots, tile, tile), BF16),
            vmem((WAYS, slots + 1, tile, tile), F32),
            vmem((span, COLS * rows, rows), BF16),
            vmem((rows, fin), BF16),
            vmem((1, rows), jnp.int32),
            vmem((fin, fh), BF16),
            vmem((1, fh), F32),
            vmem((rows, fh), BF16),
            vmem((span * slots,), jnp.int32),
            vmem((span * slots,), jnp.int32),
            vmem((1, padded), jnp.int32),
            vmem((1, 2 * padded), jnp.int32),
            pltpu.SMEM((span,), jnp.int32),
            pltpu.SMEM((1, 2 * padded), jnp.int32),
            vmem((rows, fin), F32),
            vmem((span, rows, fin), BF16),
            vmem((2, rows // 2, fin), F32),
            vmem((3, 2, rows // 2, fin), BF16),
            vmem((3, 2, rows // 2, fin), BF16),
            vmem((COLS, 2, fin, rows // 2), BF16),
            vmem((span, fin, rows), F32),
            vmem((span, fin, rows), BF16),
            vmem((span, fin, rows), BF16),
            vmem((COLS, half + 8, fin), F32),
            vmem((COLS, half + 8, fin), F32),
            vmem((2, n_xy, piece + 8, fin), F32),
            vmem((2, n_xy, piece + 8, fin), F32),
            vmem((n_z, piece + 8, fin), F32),
            vmem((COLS, n_xy, piece, fin), F32),
            dma((8,)),
            dma((span,)),
            dma,
            dma((span,)),
            dma((span,)),
            dma((3, 2)),
            dma((3, 2)),
            dma((3, 2)),
            dma((COLS, 2)),
            dma((span,)),
            dma((span,)),
            dma((2,)),
            dma((2,)),
            dma((2 * n_xy - 1,)),
            dma((2, n_xy)),
            dma((n_z - 1,)),
            dma((n_z,)),
            dma((2 * n_xy - 1,)),
            dma((2, n_xy)),
            dma((2,)),
            dma((2,)),
        ],
        compiler_params=pltpu.CompilerParams(
            collective_id=0, has_side_effects=True, vmem_limit_bytes=52 * 2**20
        ),
        name="graph_layer",
    )(*(pltpu.with_memory_space_constraint(value, pltpu.HBM) for value in inputs))
    act, gf, gw, gb = pl.pallas_call(
        deliver,
        out_shape=out_shape,
        in_specs=[anywhere] * 4,
        out_specs=(anywhere,) * 4,
        scratch_shapes=[dma((4,))],
        name="graph_results",
    )(*(pltpu.with_memory_space_constraint(value, pltpu.VMEM) for value in results))
    return act, gf, gw, gb.reshape(fh)


def solution(mesh):
    return jax.shard_map(
        local,
        mesh=mesh,
        in_specs=(
            P(("blk", "col"), None),
            P(("blk", "col")),
            P(("blk", "col"), None, None),
            P(("blk", "col")),
            P(("blk", "col")),
            P(("blk", "col")),
            P(),
            P(),
            P(("blk", "col"), None),
        ),
        out_specs=(P(("blk", "col"), None), P(("blk", "col"), None), P(), P()),
        check_vma=False,
    )
```
